256 devices in a mesh: section: 4 (over x), expert: 64 (over y, z, core).
Axes of the slice: x: 4, y: 4, z: 8, core: 2. Of those that a mesh axis runs over, the one named last changes fastest.
Arguments:
- tokens: bfloat16 [8, 1024, 2048], P('section', 'expert'), may hold values from -6 to 6
- norm_gain: float32 [4, 2048], P('section'), may hold values from 0.1 to 1.9
- gate_proj: bfloat16 [4, 64, 2048, 768], P('section', 'expert'), may hold values from -0.125 to 0.125
- up_proj: bfloat16 [4, 64, 2048, 768], P('section', 'expert'), may hold values from -0.125 to 0.125
- down_proj: bfloat16 [4, 64, 768, 2048], P('section', 'expert'), may hold values from -0.21875 to 0.21875
- expert_ids: int32 [4, 8, 1024, 8], P('section', None, 'expert'), may hold values from 0 to 63, all different within a row; in each aligned block of 16 rows (0 to 15, 16 to 31, ..., all dimensions but the last counted through in order) at most 2 rows name the same one
- gate_weights: float32 [4, 8, 1024, 8], P('section', None, 'expert'), may hold values from 0.05 to 1
Outputs:
- finished: bfloat16 [8, 1024, 2048], P('section', 'expert')
The draws below stay inside these ranges and needn't reach their ends.
Inputs may be any that keep to these rules, and one draw needn't show every extreme that they name: `expert_ids`: each row names 8 different experts. In each aligned block of 16 rows (one device's rows of one layer and micro-batch) no expert is named by more than 2 rows, and in some block one expert is named by exactly 2 rows.
All inputs are finite; a program needn't handle non-finite values.
Results may differ from the reference program's by a relative error of at most 0.015.
Values may be sent and summed in bfloat16 or wider, within the bound.
No kernel may reach another device: no remote copies, remote signals or barrier semaphores. Data moves between devices by JAX's collectives and lax.ppermute only.
A program may use at most 64 MiB of HBM per device.

```python
import math
import jax
import jax.numpy as jnp
import numpy as np
from jax import lax

D = 2048
FF = 768
TOP = 8
ROWS = 16
EXPERTS = 64
CAP = 2
MICRO = 8
TOKENS = 1024
N_SECTION = 4
N_EXPERT = 64


def shard_levels(own_key, extent, cuts, smallest, largest):
    def one(dim, shards_of):
        heights = jax.random.uniform(jax.random.fold_in(jax.random.fold_in(own_key, 6), dim), (shards_of,), jnp.float32, smallest / len(cuts), largest / len(cuts))
        return jnp.repeat(jnp.exp(heights), extent[dim] // shards_of).reshape((-1,) + (1,) * (len(extent) - dim - 1))

    gain = one(*cuts[0])
    for cut in cuts[1:]:
        gain = gain * one(*cut)
    return gain


def shared_out(stream_key, own, number, rows, amount, top, reach, slope):
    order = jax.random.permutation(stream_key, amount)
    heavy_load, common = load_shares(amount, rows * top, reach, slope, True), load_shares(amount, rows * top, reach, slope, False)
    places = jnp.arange(amount)

    def named(tallies, offset_by):
        used = int((tallies > 0).sum())
        fixed = max(1, used // 4)
        passed = fixed + (places - fixed + offset_by * (used - fixed)) % max(1, amount - fixed)
        return jnp.zeros((amount,), jnp.int32).at[order[jnp.where(places < fixed, places, passed)]].set(jnp.asarray(tallies, jnp.int32))

    tallies = jnp.where(number % 4 == 0, named(heavy_load, number // 4), named(common, number - number // 4 - 1))
    mixed = jax.random.permutation(jax.random.fold_in(own, 3), amount)
    giver, taker = mixed[0:amount // 2 * 2:2], mixed[1:amount // 2 * 2:2]
    room = jnp.minimum(tallies[giver] - 1, reach - tallies[taker]) // 2
    room = jnp.where((giver == order[0]) | (taker == order[0]) | (tallies[taker] == 0), 0, jnp.maximum(room, 0))
    passed = jax.random.randint(jax.random.fold_in(own, 4), (amount // 2,), 0, 1 << 20) % (room + 1)
    tallies = tallies.at[giver].add(-passed).at[taker].add(passed)
    labels = jnp.searchsorted(jnp.cumsum(tallies), jnp.arange(rows * top), side="right").astype(jnp.int32)
    grid = labels.reshape(top, rows).T
    grid = grid[jax.random.permutation(jax.random.fold_in(own, 1), rows)]
    offset_by = jax.random.randint(jax.random.fold_in(own, 2), (rows, 1), 0, top)
    return jnp.take_along_axis(grid, (jnp.arange(top)[None, :] + offset_by) % top, axis=1)


def load_shares(count, total, reach, skew, full):
    portions = [(1 << 20) // math.isqrt(rank ** skew) + 1 for rank in range(1, count + 1)]
    largest = reach if full else min(reach, max(-(-total // count), total * portions[0] // sum(portions)))
    least = 1 if total - largest >= count - 1 else 0
    holding, spare = [largest] + [least] * (count - 1), total - largest - least * (count - 1)
    while spare > 0:
        movable = [i for i in range(1, count) if holding[i] < largest] or [i for i in range(1, count) if holding[i] < reach]
        whole, budget = sum([portions[i] for i in movable]), spare
        for i in movable:
            addition = min(reach - holding[i], max(1, budget * portions[i] // whole), spare)
            holding[i] = holding[i] + addition
            spare = spare - addition
    return np.array(holding)


def bell_draw(key, dims, spread, reach, shards=(), kind=jnp.bfloat16):
    values = spread * jax.random.normal(key, dims, jnp.float32)
    if shards:
        values = values * shard_levels(key, dims, shards, -0.22, 0.18)
    return jnp.clip(values, -reach, reach).astype(kind)


def setup_inputs(seed: int = 0) -> dict:
    arg_keys = jax.random.split(jax.random.key(seed), 8)
    tokens = bell_draw(arg_keys[0], (MICRO, TOKENS, D), 1.0, 6.0, ((0, 4), (1, 64)))
    norm_gain = jnp.clip(1.0 + 0.18 * jax.random.normal(arg_keys[1], (N_SECTION, D), jnp.float32), 0.1, 1.9)
    gate_proj = bell_draw(arg_keys[2], (N_SECTION, EXPERTS, D, FF), D ** -0.5, 0.125, ((0, 4), (1, 64)))
    up_proj = bell_draw(arg_keys[3], (N_SECTION, EXPERTS, D, FF), D ** -0.5, 0.125, ((0, 4), (1, 64)))
    down_proj = bell_draw(arg_keys[4], (N_SECTION, EXPERTS, FF, D), FF ** -0.5, 0.21875, ((0, 4), (1, 64)))
    expert_ids_keys = jax.random.split(jax.random.fold_in(arg_keys[5], 1), N_SECTION * MICRO * TOKENS // ROWS)
    expert_ids_turns = jax.random.permutation(jax.random.fold_in(arg_keys[5], 3), N_SECTION * MICRO * TOKENS // ROWS)
    expert_ids = jax.vmap(lambda own, number: shared_out(jax.random.fold_in(arg_keys[5], 2), own, number, ROWS, EXPERTS, TOP, CAP, 2))(expert_ids_keys, expert_ids_turns).reshape((N_SECTION, MICRO, TOKENS, TOP))
    gate_weights = jnp.clip(jnp.exp(math.log(1.0) - 2.9957323 * jax.random.uniform(arg_keys[6], (N_SECTION, MICRO, TOKENS, TOP), jnp.float32) ** shard_levels(arg_keys[6], (N_SECTION, MICRO, TOKENS, TOP), ((0, 4), (2, 64)), -0.2, 0.2)), 0.05, 1.0)
    return dict(tokens=tokens, norm_gain=norm_gain, gate_proj=gate_proj, up_proj=up_proj, down_proj=down_proj, expert_ids=expert_ids, gate_weights=gate_weights)


EPSILON = 1e-06

def rms_normed(hidden, norm_scale):
    values = hidden.astype(jnp.float32)
    inverse_rms = lax.rsqrt(lax.optimization_barrier(jnp.mean(values * values, axis=-1, keepdims=True)) + EPSILON)
    return (values * inverse_rms * norm_scale.astype(jnp.float32)).astype(jnp.bfloat16)

def slot_tables(routed, expert_count, capacity):
    row_count, pick_count = routed.shape
    expert_hot = (routed[:, :, None] == jnp.arange(expert_count, dtype=jnp.int32)).astype(jnp.int32)
    flattened = expert_hot.reshape(row_count * pick_count, expert_count)
    earlier = jnp.cumsum(flattened, axis=0) - flattened
    position = lax.optimization_barrier(jnp.sum(earlier * flattened, axis=1)).reshape(row_count, pick_count).astype(jnp.int32)
    slot_hot = (position[:, :, None] == jnp.arange(capacity, dtype=jnp.int32)).astype(jnp.float32)
    placing = jnp.einsum('rke,rkc->ecr', expert_hot.astype(jnp.float32), slot_hot)
    return (placing, position)

def expert_ffn(received, w_gate, w_up, w_down):
    sources, slot_count, feature_count = received.shape
    flattened = received.reshape(sources * slot_count, feature_count)
    gate_part = jnp.dot(flattened, w_gate, preferred_element_type=jnp.float32)
    upward = jnp.dot(flattened, w_up, preferred_element_type=jnp.float32)
    activated = (jax.nn.silu(gate_part) * upward).astype(jnp.bfloat16)
    projected = jnp.dot(activated, w_down, preferred_element_type=jnp.float32).astype(jnp.bfloat16)
    return projected.reshape(sources, slot_count, feature_count)

def combine_rows(returned, routed, position, weights):
    expert_count, slot_count, feature_count = returned.shape
    flattened = returned.reshape(expert_count * slot_count, feature_count)
    slot_index = (routed * slot_count + position).reshape(-1).astype(jnp.int32)
    picked = jnp.take(flattened, slot_index, axis=0).reshape(routed.shape[0], routed.shape[1], feature_count)
    return lax.optimization_barrier(jnp.sum(picked.astype(jnp.float32) * weights[:, :, None], axis=1))

def moe_layer(hidden, norm_scale, w_gate, w_up, w_down, routed, raw_weights):
    normed = rms_normed(hidden, norm_scale).reshape(N_EXPERT, ROWS, D)
    routed_blocks = routed.reshape(N_EXPERT, ROWS, TOP)
    weights = raw_weights / lax.optimization_barrier(jnp.sum(raw_weights, axis=-1, keepdims=True))
    weight_blocks = weights.reshape(N_EXPERT, ROWS, TOP)

    def dispatch_block(pair):
        placing, position = slot_tables(pair[0], EXPERTS, CAP)
        outgoing = jnp.einsum('ecr,rd->ecd', placing, pair[1].astype(jnp.float32)).astype(jnp.bfloat16)
        return (outgoing, position)
    outgoing, positions = lax.map(dispatch_block, (routed_blocks, normed))
    received = jnp.transpose(outgoing, (1, 0, 2, 3))

    def run_expert(group):
        return expert_ffn(group[0], group[1], group[2], group[3])
    produced = lax.map(run_expert, (received, w_gate, w_up, w_down))
    returned = jnp.transpose(produced, (1, 0, 2, 3))
    combined = jax.vmap(combine_rows)(returned, routed_blocks, positions, weight_blocks)
    mixed_rows = hidden.astype(jnp.float32) + combined.reshape(TOKENS, D)
    return mixed_rows.astype(jnp.bfloat16)

def reference(tokens, norm_gain, gate_proj, up_proj, down_proj, expert_ids, gate_weights):
    results = []
    for micro_index in range(MICRO):
        entry = 2 * ((N_SECTION - micro_index) % N_SECTION) + micro_index // N_SECTION
        hidden = tokens[entry]
        for layer_index in range(N_SECTION):
            hidden = moe_layer(hidden, norm_gain[layer_index], gate_proj[layer_index], up_proj[layer_index], down_proj[layer_index], expert_ids[layer_index, micro_index], gate_weights[layer_index, micro_index])
        results.append(hidden)
    ordered = [results[(1 - slot_number % 2) * N_SECTION + N_SECTION - 1 - slot_number // 2] for slot_number in range(MICRO)]
    return jnp.stack(ordered)
```

```python
import functools

import jax
import jax.numpy as jnp
from jax import lax
from jax.experimental import pallas as pl
from jax.experimental.pallas import tpu as pltpu
from jax.sharding import PartitionSpec as P

EPSILON = 1e-06
SLOTS = 2

PAIR = (
    (3, 3, 3, 3),
    (2, 3, 3, 3),
    (0, 2, 3, 1),
    (1, 0, 2, 3),
    (1, 1, 0, 2),
    (1, 1, 1, 0),
)
RECEIVED = (
    (0, 0, 0, 0),
    (0, 0, 0, 0),
    (0, 0, 0, 1),
    (1, 0, 0, 0),
    (0, 1, 0, 0),
    (0, 0, 1, 0),
)


def normed_rows_kernel(experts, take_ref, first_ref, second_ref, gain_ref, ids_ref, hidden_ref, out_ref):
    rows = first_ref.shape[0]
    block = rows // 2
    hidden = jnp.where(take_ref[0] == 0, first_ref[...], second_ref[...])
    hidden_ref[...] = hidden
    values = hidden.astype(jnp.float32)
    inverse = lax.rsqrt(jnp.mean(values * values, axis=-1, keepdims=True) + EPSILON)
    normed = (values * inverse * gain_ref[...]).astype(jnp.bfloat16)
    height = experts * 2 * SLOTS
    place = lax.broadcasted_iota(jnp.int32, (height, rows), 0)
    source = lax.broadcasted_iota(jnp.int32, (height, rows), 1)
    expert = place // (2 * SLOTS)
    member = (place // SLOTS) % 2
    slot = place % SLOTS
    named = jnp.zeros((height, rows), jnp.bool_)
    for choice in range(ids_ref.shape[0]):
        named = jnp.logical_or(named, ids_ref[choice : choice + 1, :] == expert)
    named = jnp.logical_and(named, source // block == member)
    hot = jnp.where(named, 1.0, 0.0).astype(jnp.bfloat16)
    row = lax.broadcasted_iota(jnp.int32, (rows, rows), 0)
    column = lax.broadcasted_iota(jnp.int32, (rows, rows), 1)
    before = jnp.where(row < column, 1.0, 0.0).astype(jnp.bfloat16)
    earlier = jnp.dot(hot, before, preferred_element_type=jnp.float32)
    chosen = jnp.logical_and(named, earlier == slot.astype(jnp.float32))
    placing = jnp.where(chosen, 1.0, 0.0).astype(jnp.bfloat16)
    sent = jnp.dot(placing, normed, preferred_element_type=jnp.float32)
    out_ref[...] = sent.reshape(out_ref.shape).astype(jnp.bfloat16)


def ffn_kernel(rows_ref, gate_ref, up_ref, down_ref, out_ref, flat, total):
    step = pl.program_id(0)

    @pl.when(step == 0)
    def _():
        flat[...] = rows_ref[...].reshape(flat.shape)

    rows = flat[...]
    gate = jnp.dot(rows, gate_ref[...], preferred_element_type=jnp.float32)
    up = jnp.dot(rows, up_ref[...], preferred_element_type=jnp.float32)
    activated = (gate / (1.0 + jnp.exp(-gate)) * up).astype(jnp.bfloat16)
    part = jnp.dot(activated, down_ref[...], preferred_element_type=jnp.float32)

    @pl.when(step == 0)
    def _():
        total[...] = part

    @pl.when(jnp.logical_and(step > 0, step < pl.num_programs(0) - 1))
    def _():
        total[...] += part

    @pl.when(step == pl.num_programs(0) - 1)
    def _():
        out_ref[...] = (total[...] + part).reshape(out_ref.shape).astype(jnp.bfloat16)


def combine_kernel(experts, back_ref, hidden_ref, ids_ref, weights_ref, out_ref):
    rows = hidden_ref.shape[0]
    block = rows // 2
    width = experts * 2 * SLOTS
    raw = weights_ref[...]
    weights = raw / jnp.sum(raw, axis=-1, keepdims=True)
    source = lax.broadcasted_iota(jnp.int32, (rows, width), 0)
    place = lax.broadcasted_iota(jnp.int32, (rows, width), 1)
    expert = place // (2 * SLOTS)
    member = (place // SLOTS) % 2
    slot = place % SLOTS
    mine = source // block == member
    scale = jnp.zeros((rows, width), jnp.float32)
    named = jnp.zeros((rows, width), jnp.bool_)
    for choice in range(ids_ref.shape[1]):
        same = jnp.logical_and(ids_ref[:, choice : choice + 1] == expert, mine)
        named = jnp.logical_or(named, same)
        scale = jnp.where(same, weights[:, choice : choice + 1], scale)
    hot = jnp.where(named, 1.0, 0.0).astype(jnp.bfloat16)
    row = lax.broadcasted_iota(jnp.int32, (rows, rows), 0)
    column = lax.broadcasted_iota(jnp.int32, (rows, rows), 1)
    before = jnp.where(column < row, 1.0, 0.0).astype(jnp.bfloat16)
    earlier = jnp.dot(before, hot, preferred_element_type=jnp.float32)
    chosen = jnp.logical_and(named, earlier == slot.astype(jnp.float32))
    scale = jnp.where(chosen, scale, 0.0)
    high = scale.astype(jnp.bfloat16)
    low = (scale - high.astype(jnp.float32)).astype(jnp.bfloat16)
    back = back_ref[...].reshape(width, back_ref.shape[-1])
    mixed = jnp.dot(high, back, preferred_element_type=jnp.float32)
    mixed += jnp.dot(low, back, preferred_element_type=jnp.float32)
    out_ref[...] = (hidden_ref[...].astype(jnp.float32) + mixed).astype(jnp.bfloat16)


VMEM = pl.BlockSpec(memory_space=pltpu.VMEM)
SMEM = pl.BlockSpec(memory_space=pltpu.SMEM)
PARAMS = pltpu.CompilerParams(vmem_limit_bytes=40 * 1024 * 1024)


def normed_rows(experts, take, first, second, gain, ids):
    rows, features = first.shape
    return pl.pallas_call(
        functools.partial(normed_rows_kernel, experts),
        out_shape=(
            jax.ShapeDtypeStruct((rows, features), jnp.bfloat16),
            jax.ShapeDtypeStruct((experts, 2 * SLOTS, features), jnp.bfloat16),
        ),
        in_specs=[SMEM, VMEM, VMEM, VMEM, VMEM],
        out_specs=(VMEM, VMEM),
        compiler_params=PARAMS,
    )(take, first, second, gain, ids)


def ffn(rows, gate, up, down):
    sources, slots, features = rows.shape
    hidden_units = gate.shape[1]
    cut = 256 if hidden_units % 256 == 0 else hidden_units
    whole = pl.BlockSpec(rows.shape, lambda i: (0, 0, 0))
    return pl.pallas_call(
        ffn_kernel,
        out_shape=jax.ShapeDtypeStruct(rows.shape, jnp.bfloat16),
        grid=(hidden_units // cut,),
        in_specs=[
            whole,
            pl.BlockSpec((features, cut), lambda i: (0, i)),
            pl.BlockSpec((features, cut), lambda i: (0, i)),
            pl.BlockSpec((cut, features), lambda i: (i, 0)),
        ],
        out_specs=whole,
        scratch_shapes=[
            pltpu.VMEM((sources * slots, features), jnp.bfloat16),
            pltpu.VMEM((sources * slots, features), jnp.float32),
        ],
        compiler_params=PARAMS,
    )(rows, gate, up, down)


def combine(experts, back, hidden, ids, weights):
    return pl.pallas_call(
        functools.partial(combine_kernel, experts),
        out_shape=jax.ShapeDtypeStruct(hidden.shape, jnp.bfloat16),
        in_specs=[VMEM] * 4,
        out_specs=VMEM,
        compiler_params=PARAMS,
    )(back, hidden, ids, weights)


def on_device(tokens, norm_gain, gate_proj, up_proj, down_proj, expert_ids, gate_weights):
    section = lax.axis_index("section")
    experts = lax.axis_size("expert")
    block, features = tokens.shape[1:]
    rows = 2 * block
    own = tokens.reshape(rows, features)

    def move(value, route):
        return lax.ppermute(value, "section", route)

    def exchange(value):
        return lax.all_to_all(value, "expert", split_axis=0, concat_axis=0, tiled=True)

    back_one = [(i, (i - 1) % 4) for i in range(4)]
    on_one = [(i, (i + 1) % 4) for i in range(4)]
    arrived = move(own, [(1, 0)])
    second_in = move(own, [(2, 0)])
    ids = (expert_ids[0], move(expert_ids[0], back_one))
    raw = (gate_weights[0], move(gate_weights[0], back_one))
    gains = (norm_gain, move(norm_gain, back_one))
    own_layer = (gate_proj[0, 0], up_proj[0, 0], down_proj[0, 0])
    next_layer = tuple(move(part, back_one) for part in own_layer)

    def choice(table):
        return jnp.array(table, jnp.int32)[section]

    def of_pair(value, pair):
        low = lax.dynamic_index_in_dim(value, pair, 0, keepdims=False)
        high = lax.dynamic_index_in_dim(value, pair + 4, 0, keepdims=False)
        return jnp.concatenate([low, high], axis=0)

    def step(number, take, first, second):
        pair = choice(PAIR[number])
        received = choice(RECEIVED[number]) == 1
        if any(RECEIVED[number]):
            step_ids = of_pair(jnp.where(received, ids[1], ids[0]), pair)
            step_raw = of_pair(jnp.where(received, raw[1], raw[0]), pair)
            gain = jnp.where(received, gains[1], gains[0])
        else:
            step_ids, step_raw, gain = of_pair(ids[0], pair), of_pair(raw[0], pair), gains[0]
        hidden, sent = normed_rows(experts, take.reshape(1), first, second, gain, step_ids.T)
        gathered = exchange(sent)
        if any(RECEIVED[number]):
            made = lax.cond(
                received,
                lambda value: ffn(value, *next_layer),
                lambda value: ffn(value, *own_layer),
                gathered,
            )
        else:
            made = ffn(gathered, *own_layer)
        return combine(experts, exchange(made), hidden, step_ids, step_raw)

    keep = jnp.zeros((), jnp.int32)
    state = step(0, keep, arrived, arrived)
    state = move(state, [(0, 1)])
    state = step(1, choice((1, 0, 0, 0)), state, second_in)
    state = move(state, [(0, 1), (1, 2)])
    state = step(2, choice((1, 0, 0, 1)), state, own)
    state = move(state, on_one)
    state = step(3, keep, state, state)
    state = move(state, on_one)
    finished_first = state
    state = step(4, keep, state, state)
    finished_second = move(state, [(3, 1)])
    state = move(state, [(1, 2), (2, 3)])
    state = step(5, keep, state, state)
    state = jnp.where(section == 0, finished_first, jnp.where(section == 1, finished_second, state))
    return state.reshape(2, block, features)[::-1]


def solution(mesh):
    return jax.shard_map(
        on_device,
        mesh=mesh,
        in_specs=(
            P("section", "expert", None),
            P("section", None),
            P("section", "expert", None, None),
            P("section", "expert", None, None),
            P("section", "expert", None, None),
            P("section", None, "expert", None),
            P("section", None, "expert", None),
        ),
        out_specs=P("section", "expert", None),
        check_vma=False,
    )
```

```python
import functools

import jax
import jax.numpy as jnp
from jax import lax
from jax.experimental import pallas as pl
from jax.experimental.pallas import tpu as pltpu
from jax.sharding import PartitionSpec as P

EPSILON = 1e-06
SLOTS = 2
GROUP = 2 * SLOTS

OWN, UPPER, LOWER = 0, 1, 2

PAIRS = (
    ((2, 0, 0, 1),),
    ((0, 0, 0, 0), (3, 2, 0, 1)),
    ((0, 3, 1, 2),),
    ((2, 3, 1, 0),),
    ((3, 0, 1, 0),),
)
LAYERS = (
    (OWN, OWN, OWN, UPPER),
    (OWN, OWN, OWN, UPPER),
    (UPPER, OWN, LOWER, LOWER),
    (LOWER, UPPER, OWN, LOWER),
    (LOWER, OWN, UPPER, OWN),
)
TAKES = (
    ((1, 0, 0, 0),),
    ((0, 0, 0, 0), (1, 2, 0, 0)),
    ((1, 0, 0, 0),),
    ((0, 1, 1, 0),),
    ((0, 1, 1, 1),),
)


def looked_up(table, section):
    value = jnp.int32(table[0])
    for index in range(1, len(table)):
        value = jnp.where(section == index, jnp.int32(table[index]), value)
    return value


def picked(values, number):
    value = values[0]
    for index in range(1, len(values)):
        value = jnp.where(number == index, values[index], value)
    return value


def of_pair(refs, number, pair):
    both = [jnp.concatenate([ref[pair], ref[pair + 4]], axis=0) for ref in refs]
    return picked(both, number)


def chosen_places(ids, experts, scales=None):
    rows, choices = ids.shape
    block = rows // 2
    width = experts * GROUP
    source = lax.broadcasted_iota(jnp.int32, (rows, width), 0)
    place = lax.broadcasted_iota(jnp.int32, (rows, width), 1)
    expert = place // GROUP
    mine = source // block == (place // SLOTS) % 2
    named = jnp.zeros((rows, width), jnp.float32)
    scale = jnp.zeros((rows, width), jnp.float32)
    for choice in range(choices):
        same = jnp.logical_and(ids[:, choice : choice + 1] == expert, mine)
        named = jnp.where(same, 1.0, named)
        if scales is not None:
            scale = jnp.where(same, scales[:, choice : choice + 1], scale)
    row = lax.broadcasted_iota(jnp.int32, (rows, rows), 0)
    column = lax.broadcasted_iota(jnp.int32, (rows, rows), 1)
    before = jnp.where(column < row, 1.0, 0.0).astype(jnp.bfloat16)
    earlier = jnp.dot(before, named.astype(jnp.bfloat16), preferred_element_type=jnp.float32)
    chosen = jnp.logical_and(named > 0.0, earlier == (place % SLOTS).astype(jnp.float32))
    return jnp.where(chosen, named if scales is None else scale, 0.0)


def dispatch_kernel(step, kinds, counts, experts, section_ref, *refs):
    section = section_ref[0]
    gains, ids, refs = refs[:kinds], refs[kinds : 2 * kinds], refs[2 * kinds :]
    hidden_ref, out_ref = refs[-2:]
    layer = looked_up(LAYERS[step], section)
    gain = picked([ref[...] for ref in gains], layer)
    for lane, count in enumerate(counts):
        candidates, refs = refs[:count], refs[count:]
        hidden = picked([ref[...] for ref in candidates], looked_up(TAKES[step][lane], section))
        hidden_ref[lane] = hidden
        values = hidden.astype(jnp.float32)
        inverse = lax.rsqrt(jnp.mean(values * values, axis=-1, keepdims=True) + EPSILON)
        normed = (values * inverse * gain).astype(jnp.bfloat16)
        pair = looked_up(PAIRS[step][lane], section)
        placing = chosen_places(of_pair(ids, layer, pair), experts).T.astype(jnp.bfloat16)
        sent = jnp.dot(placing, normed, preferred_element_type=jnp.float32)
        out_ref[:, lane] = sent.astype(jnp.bfloat16).reshape(experts, GROUP, sent.shape[-1])


def in_parts(values, parts):
    total, start = None, 0
    for depth, part in parts:
        product = jnp.dot(values[:, start : start + depth], part, preferred_element_type=jnp.float32)
        total = product if total is None else total + product
        start += depth
    return total


def copy_kernel(source_ref, tie_ref, out_ref):
    out_ref[...] = source_ref[...]


def ffn_kernel(given, counts, section_ref, rows_ref, *refs):
    gates, refs = refs[: counts[0]], refs[counts[0] :]
    ups, refs = refs[: counts[1]], refs[counts[1] :]
    downs, refs = refs[: counts[2]], refs[counts[2] :]
    out_ref, activated, flat = refs[-3:]
    features = rows_ref.shape[-1]
    lanes = rows_ref.shape[1]
    units = gates[0].shape[1]
    cut = 256 if units % 256 == 0 else units
    wide = 512 if features % 512 == 0 else features
    for lane in range(lanes):
        flat[...] = rows_ref[:, lane].reshape(flat.shape)
        for start in range(0, units, cut):
            part = slice(start, start + cut)
            gate = in_parts(flat, [(ref.shape[0], ref[:, part]) for ref in gates])
            up = in_parts(flat, [(ref.shape[0], ref[:, part]) for ref in ups])
            activated[:, part] = (gate / (1.0 + jnp.exp(-gate)) * up).astype(jnp.bfloat16)
        for start in range(0, features, wide):
            part = slice(start, start + wide)
            made = in_parts(activated, [(ref.shape[0], ref[:, part]) for ref in downs])
            made = made.astype(jnp.bfloat16).reshape(out_ref.shape[0], GROUP, wide)
            if given is not None and lane == lanes - 1:
                made = jnp.where(section_ref[0] == given, refs[0][:, 0, :, part], made)
            out_ref[:, lane, :, part] = made


def combine_kernel(step, kinds, experts, last, section_ref, back_ref, hidden_ref, *refs):
    section = section_ref[0]
    ids, raw = refs[:kinds], refs[kinds : 2 * kinds]
    layer = looked_up(LAYERS[step], section)
    features = back_ref.shape[-1]
    lanes = back_ref.shape[1]
    outs = refs[-lanes:]
    for lane in range(lanes):
        pair = looked_up(PAIRS[step][lane], section)
        weights = of_pair(raw, layer, pair)
        weights = weights / jnp.sum(weights, axis=-1, keepdims=True)
        scale = chosen_places(of_pair(ids, layer, pair), experts, weights)
        high = scale.astype(jnp.bfloat16)
        low = (scale - high.astype(jnp.float32)).astype(jnp.bfloat16)
        back = back_ref[:, lane].reshape(experts * GROUP, features)
        mixed = jnp.dot(high, back, preferred_element_type=jnp.float32)
        mixed += jnp.dot(low, back, preferred_element_type=jnp.float32)
        made = (hidden_ref[lane].astype(jnp.float32) + mixed).astype(jnp.bfloat16)
        if last is None:
            outs[lane][...] = made
        else:
            made = jnp.where(section == last, refs[2 * kinds][...], made)
            block = made.shape[0] // 2
            outs[lane][0] = made[block:]
            outs[lane][1] = made[:block]


VMEM = pl.BlockSpec(memory_space=pltpu.VMEM)
SMEM = pl.BlockSpec(memory_space=pltpu.SMEM)
WHEREVER = pl.BlockSpec(memory_space=pl.ANY)


def limit(mebibytes):
    return pltpu.CompilerParams(vmem_limit_bytes=mebibytes * 1024 * 1024)


def dispatch(step, experts, section, gains, ids, lanes):
    rows, features = lanes[0][0].shape
    counts = tuple(len(lane) for lane in lanes)
    operands = (*gains, *ids, *(value for lane in lanes for value in lane))
    return pl.pallas_call(
        functools.partial(dispatch_kernel, step, len(gains), counts, experts),
        out_shape=(
            jax.ShapeDtypeStruct((len(lanes), rows, features), jnp.bfloat16),
            jax.ShapeDtypeStruct((experts, len(lanes), GROUP, features), jnp.bfloat16),
        ),
        in_specs=[SMEM] + [VMEM] * len(operands),
        out_specs=(VMEM, VMEM),
        compiler_params=limit(12),
    )(section, *operands)


def copied_after(value, tie):
    return pl.pallas_call(
        copy_kernel,
        out_shape=jax.ShapeDtypeStruct(value.shape, value.dtype),
        in_specs=[VMEM, WHEREVER],
        out_specs=VMEM,
        compiler_params=limit(12),
    )(value, tie)


def ffn(section, rows, weights, given=None, made=(), ties=()):
    sources, lanes, group, features = rows.shape
    units = weights[0][0].shape[1]
    height = sources * group
    counts = tuple(len(parts) for parts in weights)
    weights = [part for parts in weights for part in parts]
    return pl.pallas_call(
        functools.partial(ffn_kernel, given, counts),
        out_shape=jax.ShapeDtypeStruct(rows.shape, jnp.bfloat16),
        in_specs=[SMEM] + [VMEM] * (1 + len(weights) + len(made)) + [WHEREVER] * len(ties),
        out_specs=VMEM,
        scratch_shapes=[
            pltpu.VMEM((height, units), jnp.bfloat16),
            pltpu.VMEM((height, features), jnp.bfloat16),
        ],
        cost_estimate=pl.CostEstimate(
            flops=6 * lanes * height * features * units,
            bytes_accessed=6 * features * units + 4 * lanes * height * features,
            transcendentals=lanes * height * units,
        ),
        compiler_params=limit(20),
    )(section, rows, *weights, *made, *ties)


def combine(step, experts, section, back, hidden, ids, raw, ties=(), last=None, finished=()):
    lanes, rows, features = hidden.shape
    shape = (rows, features) if last is None else (2, rows // 2, features)
    operands = (back, hidden, *ids, *raw, *finished)
    return pl.pallas_call(
        functools.partial(combine_kernel, step, len(ids), experts, last),
        out_shape=tuple(jax.ShapeDtypeStruct(shape, jnp.bfloat16) for _ in range(lanes)),
        in_specs=[SMEM] + [VMEM] * len(operands) + [WHEREVER] * len(ties),
        out_specs=tuple(VMEM for _ in range(lanes)),
        compiler_params=limit(12),
    )(section, *operands, *ties)


def on_device(tokens, norm_gain, gate_proj, up_proj, down_proj, expert_ids, gate_weights):
    section = lax.axis_index("section")
    at = section.reshape(1)
    experts = lax.axis_size("expert")
    block, features = tokens.shape[1:]
    own = tokens.reshape(2 * block, features)

    def move(value, *route):
        return lax.ppermute(value, "section", route)

    def exchange(value):
        return lax.all_to_all(value, "expert", split_axis=0, concat_axis=0, tiled=True)

    downward = ((1, 0), (2, 1), (3, 2), (0, 3))
    upward = ((1, 2), (2, 3), (3, 0), (0, 1))
    small = (norm_gain, expert_ids[0], gate_weights[0])
    small_upper = tuple(move(value, *downward) for value in small)
    small_lower = tuple(move(value, *upward) for value in small)
    gains, ids, raw = zip(small, small_upper, small_lower)

    weights = ((gate_proj[0, 0],), (up_proj[0, 0],), (down_proj[0, 0],))
    gate, up, down = (jnp.split(parts[0], 2) for parts in weights)

    def layer_of(step, rows, held, ties=()):
        layer = looked_up(LAYERS[step], section)
        late = jnp.logical_and(layer == LOWER, section == 0)
        branches = [functools.partial(ffn, at, weights=value, ties=ties) for value in held]
        return lax.switch(jnp.where(late, LOWER + 1, layer), branches, rows)

    first_in = move(own, (2, 0))
    second_in = move(own, (1, 0))
    hidden, sent = dispatch(0, experts, at, gains[:2], ids[:2], [(own, first_in)])
    first = copied_after(weights[0][0], hidden)
    upper = [move(value, *downward[:3]) for value in (first, *up, *down)]
    lower_early = [move(value, *upward[:2]) for value in (first, *up, *down)]
    lower_late = [move(value, upward[2]) for value in (*gate, *up, *down)]
    rows = exchange(sent)
    away = move(rows, (3, 0))
    made = exchange(ffn(at, rows, weights))
    away = move(ffn(at, away, weights), (0, 3))
    ties = (upper[0], lower_early[0])
    (state,) = combine(0, experts, at, made, hidden, ids[:1], raw[:1], ties)
    state = move(state, (0, 1))

    hidden, sent = dispatch(1, experts, at, gains[:1], ids[:1], [(own,), (own, second_in, state)])
    rows = exchange(sent)
    ties = (upper[1], lower_early[1], lower_late[0], *small_lower, *small_upper)
    made = ffn(at, rows, weights, 3, (away,), ties)
    ties = (*upper[2:4], *lower_early[2:4], *lower_late[1:3])
    kept, state = combine(1, experts, at, exchange(made), hidden, ids[:2], raw[:2], ties)
    state = move(state, (0, 1), (1, 3), (3, 2))

    held = [weights]
    held += [(parts[:1], parts[1:3], parts[3:]) for parts in (upper, lower_early)]
    hidden, sent = dispatch(2, experts, at, gains, ids, [(state, kept)])
    rows = exchange(sent)
    made = exchange(layer_of(2, rows, held, (lower_late[3],)))
    (kept,) = combine(2, experts, at, made, hidden, ids, raw, (lower_late[4],))
    state = move(kept, (0, 3), (3, 0))

    held.append((lower_late[:2], lower_late[2:4], lower_late[4:]))
    hidden, sent = dispatch(3, experts, at, gains, ids, [(state, kept)])
    made = exchange(layer_of(3, exchange(sent), held))
    (kept,) = combine(3, experts, at, made, hidden, ids, raw)
    state = move(kept, (1, 0), (0, 1))

    hidden, sent = dispatch(4, experts, at, gains, ids, [(state, kept)])
    made = exchange(layer_of(4, exchange(sent), held))
    (finished,) = combine(4, experts, at, made, hidden, ids, raw, (), 1, (state,))
    return finished


def solution(mesh):
    return jax.shard_map(
        on_device,
        mesh=mesh,
        in_specs=(
            P("section", "expert", None),
            P("section", None),
            P("section", "expert", None, None),
            P("section", "expert", None, None),
            P("section", "expert", None, None),
            P("section", None, "expert", None),
            P("section", None, "expert", None),
        ),
        out_specs=P("section", "expert", None),
        check_vma=False,
    )
```

```python
import functools

import jax
import jax.numpy as jnp
from jax import lax
from jax.experimental import pallas as pl
from jax.experimental.pallas import tpu as pltpu
from jax.sharding import PartitionSpec as P

EPSILON = 1e-06
SLOTS = 2
GROUP = 2 * SLOTS

OWN, UPPER, LOWER = 0, 1, 2

PAIRS = (
    ((2, 0, 0, 1),),
    ((0, 0, 0, 0), (3, 2, 0, 1)),
    ((0, 3, 1, 2),),
    ((2, 3, 1, 0),),
    ((3, 0, 1, 0),),
)
LAYERS = (
    (OWN, OWN, OWN, UPPER),
    (OWN, OWN, OWN, UPPER),
    (UPPER, OWN, LOWER, LOWER),
    (LOWER, UPPER, OWN, LOWER),
    (LOWER, OWN, UPPER, OWN),
)
TAKES = (
    ((1, 0, 0, 0),),
    ((0, 0, 0, 0), (1, 2, 0, 0)),
    ((1, 0, 0, 0),),
    ((0, 1, 1, 0),),
    ((0, 1, 1, 1),),
)


def looked_up(table, section):
    value = jnp.int32(table[0])
    for index in range(1, len(table)):
        value = jnp.where(section == index, jnp.int32(table[index]), value)
    return value


def picked(values, number):
    value = values[0]
    for index in range(1, len(values)):
        value = jnp.where(number == index, values[index], value)
    return value


def of_pair(refs, number, pair):
    both = [jnp.concatenate([ref[pair], ref[pair + 4]], axis=0) for ref in refs]
    return picked(both, number)


def chosen_places(ids, experts, scales=None):
    rows, choices = ids.shape
    block = rows // 2
    width = experts * GROUP
    source = lax.broadcasted_iota(jnp.int32, (rows, width), 0)
    place = lax.broadcasted_iota(jnp.int32, (rows, width), 1)
    expert = place // GROUP
    mine = source // block == (place // SLOTS) % 2
    named = jnp.zeros((rows, width), jnp.float32)
    scale = jnp.zeros((rows, width), jnp.float32)
    for choice in range(choices):
        same = jnp.logical_and(ids[:, choice : choice + 1] == expert, mine)
        named = jnp.where(same, 1.0, named)
        if scales is not None:
            scale = jnp.where(same, scales[:, choice : choice + 1], scale)
    row = lax.broadcasted_iota(jnp.int32, (rows, rows), 0)
    column = lax.broadcasted_iota(jnp.int32, (rows, rows), 1)
    before = jnp.where(column < row, 1.0, 0.0).astype(jnp.bfloat16)
    earlier = jnp.dot(before, named.astype(jnp.bfloat16), preferred_element_type=jnp.float32)
    chosen = jnp.logical_and(named > 0.0, earlier == (place % SLOTS).astype(jnp.float32))
    return jnp.where(chosen, named if scales is None else scale, 0.0)


def dispatch_kernel(step, kinds, counts, experts, section_ref, *refs):
    section = section_ref[0]
    gains, ids, refs = refs[:kinds], refs[kinds : 2 * kinds], refs[2 * kinds :]
    hidden_ref, out_ref = refs[-2:]
    layer = looked_up(LAYERS[step], section)
    gain = picked([ref[...] for ref in gains], layer)
    for lane, count in enumerate(counts):
        candidates, refs = refs[:count], refs[count:]
        hidden = picked([ref[...] for ref in candidates], looked_up(TAKES[step][lane], section))
        hidden_ref[lane] = hidden
        values = hidden.astype(jnp.float32)
        inverse = lax.rsqrt(jnp.mean(values * values, axis=-1, keepdims=True) + EPSILON)
        normed = (values * inverse * gain).astype(jnp.bfloat16)
        pair = looked_up(PAIRS[step][lane], section)
        placing = chosen_places(of_pair(ids, layer, pair), experts).T.astype(jnp.bfloat16)
        sent = jnp.dot(placing, normed, preferred_element_type=jnp.float32)
        out_ref[:, lane] = sent.astype(jnp.bfloat16).reshape(experts, GROUP, sent.shape[-1])


def pieces(features, units, width):
    panels = units // width
    order = [number for panel in range(panels) for number in (panel, panels + panel)]
    spans = [(number * features, features) for number in order]
    each = units * (2 if features // width % 2 == 0 else 1)
    first = 2 * panels * features
    return spans + [(start, each) for start in range(first, first + units * features // width, each)]


def pack_kernel(width, *refs):
    gate_ref, up_ref, down_ref = refs[:3]
    out_ref, done = refs[-2:]
    features, units = gate_ref.shape
    copies, start = [], 0
    for ref in (gate_ref, up_ref, down_ref):
        for column in range(0, ref.shape[1], width):
            to = out_ref.at[pl.ds(start, ref.shape[0]), :]
            copies.append(pltpu.make_async_copy(ref.at[:, pl.ds(column, width)], to, done.at[len(copies)]))
            start += ref.shape[0]
    for copy in copies:
        copy.start()
    for copy in copies:
        copy.wait()


def ffn_kernel(step, given, held, section_ref, rows_ref, *refs):
    layers, refs = refs[:held], refs[held:]
    out_ref, weights, activated, flat, arrived = refs[-5:]
    experts, lanes, _, features = rows_ref.shape
    units = activated.shape[-1]
    width = weights.shape[1]
    panels = units // width
    section = section_ref[0]
    spans = pieces(features, units, width)

    def copies(ref):
        for number, (start, size) in enumerate(spans):
            rows = pl.ds(start, size)
            yield pltpu.make_async_copy(ref.at[rows, :], weights.at[rows, :], arrived.at[number])

    if held == 1:
        for copy in copies(layers[0]):
            copy.start()
    else:
        layer = looked_up(LAYERS[step], section)
        layer = jnp.where(jnp.logical_and(layer == LOWER, section == 0), LOWER + 1, layer)
        for number, ref in enumerate(layers):

            @pl.when(layer == number)
            def _(ref=ref):
                for copy in copies(ref):
                    copy.start()

    def arrival(number, start, size):
        rows = pl.ds(pl.multiple_of(start, width), size)
        pltpu.make_async_copy(layers[0].at[rows, :], weights.at[rows, :], arrived.at[number]).wait()

    for lane in range(lanes):
        flat[lane] = rows_ref[:, lane].reshape(flat.shape[1:])

    def widen(panel, _):
        start = panel * features
        arrival(2 * panel, start, features)
        arrival(2 * panel + 1, start + panels * features, features)
        gates = weights[pl.ds(pl.multiple_of(start, width), features)]
        ups = weights[pl.ds(pl.multiple_of(start + panels * features, width), features)]
        part = pl.ds(pl.multiple_of(panel * width, width), width)
        for lane in range(lanes):
            gate = jnp.dot(flat[lane], gates, preferred_element_type=jnp.float32)
            up = jnp.dot(flat[lane], ups, preferred_element_type=jnp.float32)
            activated[lane, :, part] = (gate / (1.0 + jnp.exp(-gate)) * up).astype(jnp.bfloat16)
        return 0

    lax.fori_loop(0, panels, widen, 0)
    size = spans[-1][1]

    def narrow(number, _):
        first = 2 * panels * features + number * size
        arrival(2 * panels + number, first, size)
        for inner in range(size // units):
            down = weights[pl.ds(pl.multiple_of(first + inner * units, width), units)]
            column = (number * (size // units) + inner) * width
            part = pl.ds(pl.multiple_of(column, width), width)
            for lane in range(lanes):
                made = jnp.dot(activated[lane], down, preferred_element_type=jnp.float32)
                made = made.astype(jnp.bfloat16).reshape(experts, GROUP, width)
                if given is not None and lane == lanes - 1:
                    made = jnp.where(section == given, refs[0][:, 0, :, part], made)
                out_ref[:, lane, :, part] = made
        return 0

    lax.fori_loop(0, len(spans) - 2 * panels, narrow, 0)


def combine_kernel(step, kinds, experts, last, section_ref, back_ref, hidden_ref, *refs):
    section = section_ref[0]
    ids, raw = refs[:kinds], refs[kinds : 2 * kinds]
    layer = looked_up(LAYERS[step], section)
    features = back_ref.shape[-1]
    lanes = back_ref.shape[1]
    outs = refs[-lanes:]
    for lane in range(lanes):
        pair = looked_up(PAIRS[step][lane], section)
        weights = of_pair(raw, layer, pair)
        weights = weights / jnp.sum(weights, axis=-1, keepdims=True)
        scale = chosen_places(of_pair(ids, layer, pair), experts, weights)
        high = scale.astype(jnp.bfloat16)
        low = (scale - high.astype(jnp.float32)).astype(jnp.bfloat16)
        back = back_ref[:, lane].reshape(experts * GROUP, features)
        mixed = jnp.dot(high, back, preferred_element_type=jnp.float32)
        mixed += jnp.dot(low, back, preferred_element_type=jnp.float32)
        made = (hidden_ref[lane].astype(jnp.float32) + mixed).astype(jnp.bfloat16)
        if last is None:
            outs[lane][...] = made
        else:
            made = jnp.where(section == last, refs[2 * kinds][...], made)
            block = made.shape[0] // 2
            outs[lane][0] = made[block:]
            outs[lane][1] = made[:block]


VMEM = pl.BlockSpec(memory_space=pltpu.VMEM)
SMEM = pl.BlockSpec(memory_space=pltpu.SMEM)
WHEREVER = pl.BlockSpec(memory_space=pl.ANY)


def limit(mebibytes):
    return pltpu.CompilerParams(vmem_limit_bytes=mebibytes * 1024 * 1024)


def dispatch(step, experts, section, gains, ids, lanes, ties=()):
    rows, features = lanes[0][0].shape
    counts = tuple(len(lane) for lane in lanes)
    operands = (*gains, *ids, *(value for lane in lanes for value in lane))
    return pl.pallas_call(
        functools.partial(dispatch_kernel, step, len(gains), counts, experts),
        out_shape=(
            jax.ShapeDtypeStruct((len(lanes), rows, features), jnp.bfloat16),
            jax.ShapeDtypeStruct((experts, len(lanes), GROUP, features), jnp.bfloat16),
        ),
        in_specs=[SMEM] + [VMEM] * len(operands) + [WHEREVER] * len(ties),
        out_specs=(VMEM, VMEM),
        compiler_params=limit(12),
    )(section, *operands, *ties)


def packed(gate, up, down, ties):
    features, units = gate.shape
    width = 256 if units % 256 == 0 and features % 256 == 0 else units
    return pl.pallas_call(
        functools.partial(pack_kernel, width),
        out_shape=jax.ShapeDtypeStruct((3 * features * units // width, width), gate.dtype),
        in_specs=[WHEREVER] * (3 + len(ties)),
        out_specs=WHEREVER,
        scratch_shapes=[pltpu.SemaphoreType.DMA((2 * units // width + features // width,))],
        compiler_params=limit(4),
    )(gate, up, down, *ties)


def ffn(step, section, rows, layers, given=None, made=(), ties=()):
    experts, lanes, group, features = rows.shape
    length, width = layers[0].shape
    units = length * width // (3 * features)
    height = experts * group
    return pl.pallas_call(
        functools.partial(ffn_kernel, step, given, len(layers)),
        out_shape=jax.ShapeDtypeStruct(rows.shape, jnp.bfloat16),
        in_specs=[SMEM, VMEM] + [WHEREVER] * len(layers) + [VMEM] * len(made) + [WHEREVER] * len(ties),
        out_specs=VMEM,
        scratch_shapes=[
            pltpu.VMEM((length, width), jnp.bfloat16),
            pltpu.VMEM((lanes, height, units), jnp.bfloat16),
            pltpu.VMEM((lanes, height, features), jnp.bfloat16),
            pltpu.SemaphoreType.DMA((len(pieces(features, units, width)),)),
        ],
        cost_estimate=pl.CostEstimate(
            flops=6 * lanes * height * features * units,
            bytes_accessed=6 * features * units + 4 * lanes * height * features,
            transcendentals=lanes * height * units,
        ),
        compiler_params=limit(28),
    )(section, rows, *layers, *made, *ties)


def combine(step, experts, section, back, hidden, ids, raw, ties=(), last=None, finished=()):
    lanes, rows, features = hidden.shape
    shape = (rows, features) if last is None else (2, rows // 2, features)
    operands = (back, hidden, *ids, *raw, *finished)
    return pl.pallas_call(
        functools.partial(combine_kernel, step, len(ids), experts, last),
        out_shape=tuple(jax.ShapeDtypeStruct(shape, jnp.bfloat16) for _ in range(lanes)),
        in_specs=[SMEM] + [VMEM] * len(operands) + [WHEREVER] * len(ties),
        out_specs=tuple(VMEM for _ in range(lanes)),
        compiler_params=limit(12),
    )(section, *operands, *ties)


def on_device(tokens, norm_gain, gate_proj, up_proj, down_proj, expert_ids, gate_weights):
    section = lax.axis_index("section")
    at = section.reshape(1)
    experts = lax.axis_size("expert")
    block, features = tokens.shape[1:]
    own = tokens.reshape(2 * block, features)

    def move(value, *route):
        return lax.ppermute(value, "section", route)

    def exchange(value):
        return lax.all_to_all(value, "expert", split_axis=0, concat_axis=0, tiled=True)

    downward = ((1, 0), (2, 1), (3, 2), (0, 3))
    upward = ((1, 2), (2, 3), (3, 0), (0, 1))
    small = (norm_gain, expert_ids[0], gate_weights[0])
    small_upper = tuple(move(value, *downward) for value in small)
    small_lower = tuple(move(value, *upward) for value in small)
    gains, ids, raw = zip(small, small_upper, small_lower)

    weights = (gate_proj[0, 0], up_proj[0, 0], down_proj[0, 0])

    first_in = move(own, (2, 0))
    second_in = move(own, (1, 0))
    hidden, sent = dispatch(0, experts, at, gains[:2], ids[:2], [(own, first_in)])
    layer = packed(*weights, (hidden, second_in, *small_upper, *small_lower))
    upper = move(layer, *downward[:3])
    lower_early = move(layer, *upward[:2])
    rows = exchange(sent)
    away = move(rows, (3, 0))
    made = exchange(ffn(0, at, rows, [layer]))
    (state,) = combine(0, experts, at, made, hidden, ids[:1], raw[:1], (away,))
    state = move(state, (0, 1))

    lower_late = move(packed(*weights, (away,)), upward[2])
    away = move(ffn(0, at, away, [layer]), (0, 3))
    hidden, sent = dispatch(1, experts, at, gains[:1], ids[:1], [(own,), (own, second_in, state)])
    made = ffn(1, at, exchange(sent), [layer], 3, (away,))
    kept, state = combine(1, experts, at, exchange(made), hidden, ids[:2], raw[:2])
    state = move(state, (0, 1), (1, 3), (3, 2))

    layers = [layer, upper, lower_early]
    hidden, sent = dispatch(2, experts, at, gains, ids, [(state, kept)], layers[1:])
    made = exchange(ffn(2, at, exchange(sent), layers))
    (kept,) = combine(2, experts, at, made, hidden, ids, raw)
    state = move(kept, (0, 3), (3, 0))

    layers.append(lower_late)
    hidden, sent = dispatch(3, experts, at, gains, ids, [(state, kept)], layers[3:])
    made = exchange(ffn(3, at, exchange(sent), layers))
    (kept,) = combine(3, experts, at, made, hidden, ids, raw)
    state = move(kept, (1, 0), (0, 1))

    hidden, sent = dispatch(4, experts, at, gains, ids, [(state, kept)])
    made = exchange(ffn(4, at, exchange(sent), layers))
    (finished,) = combine(4, experts, at, made, hidden, ids, raw, (), 1, (state,))
    return finished


def solution(mesh):
    return jax.shard_map(
        on_device,
        mesh=mesh,
        in_specs=(
            P("section", "expert", None),
            P("section", None),
            P("section", "expert", None, None),
            P("section", "expert", None, None),
            P("section", "expert", None, None),
            P("section", None, "expert", None),
            P("section", None, "expert", None),
        ),
        out_specs=P("section", "expert", None),
        check_vma=False,
    )
```

```python
import functools

import jax
import jax.numpy as jnp
from jax import lax
from jax.experimental import pallas as pl
from jax.experimental.pallas import tpu as pltpu
from jax.sharding import PartitionSpec as P

EPSILON = 1e-06
LONG, LONGER = 20_000_000_000, 60_000_000_000
SLOTS = 2
GROUP = 2 * SLOTS

OWN, UPPER, LOWER = 0, 1, 2

PAIRS = (
    ((2, 0, 0, 1),),
    ((0, 0, 0, 0), (3, 2, 0, 1)),
    ((0, 3, 1, 2),),
    ((2, 3, 1, 0),),
    ((3, 0, 1, 0),),
)
LAYERS = (
    (OWN, OWN, OWN, UPPER),
    (OWN, OWN, OWN, UPPER),
    (UPPER, OWN, LOWER, LOWER),
    (LOWER, UPPER, OWN, LOWER),
    (LOWER, OWN, UPPER, OWN),
)
TAKES = (
    ((1, 0, 0, 0),),
    ((0, 0, 0, 0), (1, 2, 0, 0)),
    ((1, 0, 0, 0),),
    ((0, 1, 1, 0),),
    ((0, 1, 1, 1),),
)


def looked_up(table, section):
    value = jnp.int32(table[0])
    for index in range(1, len(table)):
        value = jnp.where(section == index, jnp.int32(table[index]), value)
    return value


def picked(values, number):
    value = values[0]
    for index in range(1, len(values)):
        value = jnp.where(number == index, values[index], value)
    return value


def of_pair(refs, number, pair):
    both = [jnp.concatenate([ref[pair], ref[pair + 4]], axis=0) for ref in refs]
    return picked(both, number)


def chosen_places(ids, experts, scales=None):
    rows, choices = ids.shape
    block = rows // 2
    width = experts * GROUP
    source = lax.broadcasted_iota(jnp.int32, (rows, width), 0)
    place = lax.broadcasted_iota(jnp.int32, (rows, width), 1)
    expert = place // GROUP
    mine = source // block == (place // SLOTS) % 2
    named = jnp.zeros((rows, width), jnp.float32)
    scale = jnp.zeros((rows, width), jnp.float32)
    for choice in range(choices):
        same = jnp.logical_and(ids[:, choice : choice + 1] == expert, mine)
        named = jnp.where(same, 1.0, named)
        if scales is not None:
            scale = jnp.where(same, scales[:, choice : choice + 1], scale)
    row = lax.broadcasted_iota(jnp.int32, (rows, rows), 0)
    column = lax.broadcasted_iota(jnp.int32, (rows, rows), 1)
    before = jnp.where(column < row, 1.0, 0.0).astype(jnp.bfloat16)
    earlier = jnp.dot(before, named.astype(jnp.bfloat16), preferred_element_type=jnp.float32)
    chosen = jnp.logical_and(named > 0.0, earlier == (place % SLOTS).astype(jnp.float32))
    return jnp.where(chosen, named if scales is None else scale, 0.0)


def dispatch_kernel(step, kinds, counts, experts, section_ref, *refs):
    section = section_ref[0]
    gains, ids, refs = refs[:kinds], refs[kinds : 2 * kinds], refs[2 * kinds :]
    hidden_ref, out_ref = refs[-2:]
    layer = looked_up(LAYERS[step], section)
    gain = picked([ref[...] for ref in gains], layer)
    for lane, count in enumerate(counts):
        candidates, refs = refs[:count], refs[count:]
        hidden = picked([ref[...] for ref in candidates], looked_up(TAKES[step][lane], section))
        hidden_ref[lane] = hidden
        values = hidden.astype(jnp.float32)
        inverse = lax.rsqrt(jnp.mean(values * values, axis=-1, keepdims=True) + EPSILON)
        normed = (values * inverse * gain).astype(jnp.bfloat16)
        pair = looked_up(PAIRS[step][lane], section)
        placing = chosen_places(of_pair(ids, layer, pair), experts).T.astype(jnp.bfloat16)
        sent = jnp.dot(placing, normed, preferred_element_type=jnp.float32)
        out_ref[:, lane] = sent.astype(jnp.bfloat16).reshape(experts, GROUP, sent.shape[-1])


def pieces(features, units, width):
    panels = units // width
    order = [number for panel in range(panels) for number in (panel, panels + panel)]
    spans = [(number * features, features) for number in order]
    first = 2 * panels * features
    return spans + [(first + panel * units, units) for panel in range(features // width)]


def spread(refs, start, size):
    for ref in refs:
        if start < ref.shape[0]:
            return ref.at[pl.ds(start, size), :]
        start -= ref.shape[0]


def pack_kernel(width, outputs, *refs):
    out_refs, done = refs[-1 - outputs : -1], refs[-1]
    copies, start = [], 0
    for ref in refs[:3]:
        for column in range(0, ref.shape[1], width):
            to = spread(out_refs, start, ref.shape[0])
            copies.append(pltpu.make_async_copy(ref.at[:, pl.ds(column, width)], to, done.at[len(copies)]))
            start += ref.shape[0]
    for copy in copies:
        copy.start()
    for copy in copies:
        copy.wait()


def ffn_kernel(step, given, held, section_ref, rows_ref, *refs):
    layers, refs = [refs[2 * number : 2 * number + 2] for number in range(held)], refs[2 * held :]
    out_ref, weights, activated, flat, arrived = refs[-5:]
    experts, lanes, _, features = rows_ref.shape
    units = activated.shape[-1]
    width = weights.shape[1]
    panels = units // width
    section = section_ref[0]
    spans = pieces(features, units, width)

    def copies(parts):
        for number, (start, size) in enumerate(spans):
            to = weights.at[pl.ds(start, size), :]
            yield pltpu.make_async_copy(spread(parts, start, size), to, arrived.at[number])

    if held == 1:
        for copy in copies(layers[0]):
            copy.start()
    else:
        layer = looked_up(LAYERS[step], section)
        layer = jnp.where(jnp.logical_and(layer == LOWER, section == 0), LOWER + 1, layer)
        for number, held_parts in enumerate(layers):

            @pl.when(layer == number)
            def _(held_parts=held_parts):
                for copy in copies(held_parts):
                    copy.start()

    def arrival(number, start, size):
        to = weights.at[pl.ds(pl.multiple_of(start, width), size), :]
        pltpu.make_async_copy(to, to, arrived.at[number]).wait()

    for lane in range(lanes):
        flat[lane] = rows_ref[:, lane].reshape(flat.shape[1:])

    def widen(panel, _):
        start = panel * features
        arrival(2 * panel, start, features)
        arrival(2 * panel + 1, start + panels * features, features)
        gates = weights[pl.ds(pl.multiple_of(start, width), features)]
        ups = weights[pl.ds(pl.multiple_of(start + panels * features, width), features)]
        part = pl.ds(pl.multiple_of(panel * width, width), width)
        for lane in range(lanes):
            gate = jnp.dot(flat[lane], gates, preferred_element_type=jnp.float32)
            up = jnp.dot(flat[lane], ups, preferred_element_type=jnp.float32)
            activated[lane, :, part] = (gate / (1.0 + jnp.exp(-gate)) * up).astype(jnp.bfloat16)
        return 0

    lax.fori_loop(0, panels, widen, 0)
    def narrow(panel, _):
        first = 2 * panels * features + panel * units
        arrival(2 * panels + panel, first, units)
        down = weights[pl.ds(pl.multiple_of(first, width), units)]
        part = pl.ds(pl.multiple_of(panel * width, width), width)
        for lane in range(lanes):
            made = jnp.dot(activated[lane], down, preferred_element_type=jnp.float32)
            made = made.astype(jnp.bfloat16).reshape(experts, GROUP, width)
            if given is not None and lane == lanes - 1:
                made = jnp.where(section == given, refs[0][:, 0, :, part], made)
            out_ref[:, lane, :, part] = made
        return 0

    lax.fori_loop(0, features // width, narrow, 0)


def combine_kernel(step, kinds, experts, last, section_ref, back_ref, hidden_ref, *refs):
    section = section_ref[0]
    ids, raw = refs[:kinds], refs[kinds : 2 * kinds]
    layer = looked_up(LAYERS[step], section)
    features = back_ref.shape[-1]
    lanes = back_ref.shape[1]
    outs = refs[-lanes:]
    for lane in range(lanes):
        pair = looked_up(PAIRS[step][lane], section)
        weights = of_pair(raw, layer, pair)
        weights = weights / jnp.sum(weights, axis=-1, keepdims=True)
        scale = chosen_places(of_pair(ids, layer, pair), experts, weights)
        high = scale.astype(jnp.bfloat16)
        low = (scale - high.astype(jnp.float32)).astype(jnp.bfloat16)
        back = back_ref[:, lane].reshape(experts * GROUP, features)
        mixed = jnp.dot(high, back, preferred_element_type=jnp.float32)
        mixed += jnp.dot(low, back, preferred_element_type=jnp.float32)
        made = (hidden_ref[lane].astype(jnp.float32) + mixed).astype(jnp.bfloat16)
        if last is None:
            outs[lane][...] = made
        else:
            made = jnp.where(section == last, refs[2 * kinds][...], made)
            block = made.shape[0] // 2
            outs[lane][0] = made[block:]
            outs[lane][1] = made[:block]


VMEM = pl.BlockSpec(memory_space=pltpu.VMEM)
SMEM = pl.BlockSpec(memory_space=pltpu.SMEM)
WHEREVER = pl.BlockSpec(memory_space=pl.ANY)


def limit(mebibytes):
    return pltpu.CompilerParams(vmem_limit_bytes=mebibytes * 1024 * 1024)


def dispatch(step, experts, section, gains, ids, lanes, ties=()):
    rows, features = lanes[0][0].shape
    counts = tuple(len(lane) for lane in lanes)
    operands = (*gains, *ids, *(value for lane in lanes for value in lane))
    return pl.pallas_call(
        functools.partial(dispatch_kernel, step, len(gains), counts, experts),
        out_shape=(
            jax.ShapeDtypeStruct((len(lanes), rows, features), jnp.bfloat16),
            jax.ShapeDtypeStruct((experts, len(lanes), GROUP, features), jnp.bfloat16),
        ),
        in_specs=[SMEM] + [VMEM] * len(operands) + [WHEREVER] * len(ties),
        out_specs=(VMEM, VMEM),
        compiler_params=limit(12),
    )(section, *operands, *ties)


def token_kernel(*refs):
    refs[-1][...] = jnp.zeros_like(refs[-1])


def arrived_token(flops, *values):
    return pl.pallas_call(
        token_kernel,
        out_shape=jax.ShapeDtypeStruct((8, 128), jnp.float32),
        in_specs=[WHEREVER] * len(values),
        out_specs=VMEM,
        cost_estimate=pl.CostEstimate(flops=flops, bytes_accessed=4096, transcendentals=0),
        compiler_params=limit(4),
    )(*values)


def packed(gate, up, down, ties):
    features, units = gate.shape
    width = 256 if units % 256 == 0 and features % 256 == 0 else units
    panels = features // width
    ahead = panels - panels * 3 // 8
    rows = (2 * features * units // width + ahead * units, (panels - ahead) * units)
    return pl.pallas_call(
        functools.partial(pack_kernel, width, 2),
        out_shape=tuple(jax.ShapeDtypeStruct((count, width), gate.dtype) for count in rows),
        in_specs=[WHEREVER] * (3 + len(ties)),
        out_specs=(WHEREVER, WHEREVER),
        scratch_shapes=[pltpu.SemaphoreType.DMA((2 * units // width + panels,))],
        compiler_params=limit(4),
    )(gate, up, down, *ties)


def ffn(step, section, rows, layers, given=None, made=(), ties=()):
    experts, lanes, group, features = rows.shape
    width = layers[0][0].shape[1]
    length = sum(part.shape[0] for part in layers[0])
    held = len(layers)
    layers = [part for parts in layers for part in parts]
    units = length * width // (3 * features)
    height = experts * group
    return pl.pallas_call(
        functools.partial(ffn_kernel, step, given, held),
        out_shape=jax.ShapeDtypeStruct(rows.shape, jnp.bfloat16),
        in_specs=[SMEM, VMEM] + [WHEREVER] * len(layers) + [VMEM] * len(made) + [WHEREVER] * len(ties),
        out_specs=VMEM,
        scratch_shapes=[
            pltpu.VMEM((length, width), jnp.bfloat16),
            pltpu.VMEM((lanes, height, units), jnp.bfloat16),
            pltpu.VMEM((lanes, height, features), jnp.bfloat16),
            pltpu.SemaphoreType.DMA((len(pieces(features, units, width)),)),
        ],
        cost_estimate=pl.CostEstimate(
            flops=6 * lanes * height * features * units,
            bytes_accessed=6 * features * units + 4 * lanes * height * features,
            transcendentals=lanes * height * units,
        ),
        compiler_params=limit(28),
    )(section, rows, *layers, *made, *ties)


def combine(step, experts, section, back, hidden, ids, raw, ties=(), last=None, finished=()):
    lanes, rows, features = hidden.shape
    shape = (rows, features) if last is None else (2, rows // 2, features)
    operands = (back, hidden, *ids, *raw, *finished)
    return pl.pallas_call(
        functools.partial(combine_kernel, step, len(ids), experts, last),
        out_shape=tuple(jax.ShapeDtypeStruct(shape, jnp.bfloat16) for _ in range(lanes)),
        in_specs=[SMEM] + [VMEM] * len(operands) + [WHEREVER] * len(ties),
        out_specs=tuple(VMEM for _ in range(lanes)),
        compiler_params=limit(12),
    )(section, *operands, *ties)


def on_device(tokens, norm_gain, gate_proj, up_proj, down_proj, expert_ids, gate_weights):
    section = lax.axis_index("section")
    at = section.reshape(1)
    experts = lax.axis_size("expert")
    block, features = tokens.shape[1:]
    own = tokens.reshape(2 * block, features)

    def move(value, *route):
        return lax.ppermute(value, "section", route)

    def exchange(value):
        return lax.all_to_all(value, "expert", split_axis=0, concat_axis=0, tiled=True)

    downward = ((1, 0), (2, 1), (3, 2), (0, 3))
    upward = ((1, 2), (2, 3), (3, 0), (0, 1))
    small = (norm_gain, expert_ids[0], gate_weights[0])
    small_upper = tuple(move(value, *downward) for value in small)
    small_lower = tuple(move(value, *upward) for value in small)
    gains, ids, raw = zip(small, small_upper, small_lower)

    weights = (gate_proj[0, 0], up_proj[0, 0], down_proj[0, 0])

    first_in = move(own, (2, 0))
    second_in = move(own, (1, 0))
    hidden, sent = dispatch(0, experts, at, gains[:2], ids[:2], [(own, first_in)])
    layer = packed(*weights, (hidden, second_in, *small_upper, *small_lower))
    upper = [move(part, *downward[:3]) for part in layer]
    lower_early = [move(part, *upward[:2]) for part in layer]
    lower_late = [move(part, upward[2]) for part in layer]
    rows = exchange(sent)
    away = move(rows, (3, 0))
    made = exchange(ffn(0, at, rows, [layer]))
    (state,) = combine(0, experts, at, made, hidden, ids[:1], raw[:1], (away,))
    state = move(state, (0, 1))

    away = move(ffn(0, at, away, [layer]), (0, 3))
    hidden, sent = dispatch(1, experts, at, gains[:1], ids[:1], [(own,), (own, second_in, state)])
    made = ffn(1, at, exchange(sent), [layer], 3, (away,))
    here = arrived_token(LONGER, upper[0], lower_early[0])
    kept, state = combine(1, experts, at, exchange(made), hidden, ids[:2], raw[:2], (here,))
    state = move(state, (0, 1), (1, 3), (3, 2))

    layers = [layer, upper, lower_early]
    hidden, sent = dispatch(2, experts, at, gains, ids, [(state, kept)])
    made = exchange(ffn(2, at, exchange(sent), layers))
    here = arrived_token(LONG, *lower_late)
    (kept,) = combine(2, experts, at, made, hidden, ids, raw, (here,))
    state = move(kept, (0, 3), (3, 0))

    layers.append(lower_late)
    hidden, sent = dispatch(3, experts, at, gains, ids, [(state, kept)])
    made = exchange(ffn(3, at, exchange(sent), layers))
    (kept,) = combine(3, experts, at, made, hidden, ids, raw)
    state = move(kept, (1, 0), (0, 1))

    hidden, sent = dispatch(4, experts, at, gains, ids, [(state, kept)])
    made = exchange(ffn(4, at, exchange(sent), layers))
    (finished,) = combine(4, experts, at, made, hidden, ids, raw, (), 1, (state,))
    return finished


def solution(mesh):
    return jax.shard_map(
        on_device,
        mesh=mesh,
        in_specs=(
            P("section", "expert", None),
            P("section", None),
            P("section", "expert", None, None),
            P("section", "expert", None, None),
            P("section", "expert", None, None),
            P("section", None, "expert", None),
            P("section", None, "expert", None),
        ),
        out_specs=P("section", "expert", None),
        check_vma=False,
    )
```

```python
import functools

import jax
import jax.numpy as jnp
from jax import lax
from jax.experimental import pallas as pl
from jax.experimental.pallas import tpu as pltpu
from jax.sharding import PartitionSpec as P

EPSILON = 1e-06
LONG, LONGER = 20_000_000_000, 60_000_000_000
SLOTS = 2
GROUP = 2 * SLOTS

OWN, UPPER, LOWER = 0, 1, 2

PAIRS = (
    ((2, 0, 0, 1),),
    ((0, 0, 0, 0), (3, 2, 0, 1)),
    ((0, 3, 1, 2),),
    ((2, 3, 1, 0),),
    ((3, 0, 1, 0),),
)
LAYERS = (
    (OWN, OWN, OWN, UPPER),
    (OWN, OWN, OWN, UPPER),
    (UPPER, OWN, LOWER, LOWER),
    (LOWER, UPPER, OWN, LOWER),
    (LOWER, OWN, UPPER, OWN),
)
TAKES = (
    ((1, 0, 0, 0),),
    ((0, 0, 0, 0), (1, 2, 0, 0)),
    ((1, 0, 0, 0),),
    ((0, 1, 1, 0),),
    ((0, 1, 1, 1),),
)


def looked_up(table, section):
    value = jnp.int32(table[0])
    for index in range(1, len(table)):
        value = jnp.where(section == index, jnp.int32(table[index]), value)
    return value


def picked(values, number):
    value = values[0]
    for index in range(1, len(values)):
        value = jnp.where(number == index, values[index], value)
    return value


def of_pair(refs, number, pair):
    both = [jnp.concatenate([ref[pair], ref[pair + 4]], axis=0) for ref in refs]
    return picked(both, number)


def chosen_places(ids, experts, scales=None):
    rows, choices = ids.shape
    block = rows // 2
    width = experts * GROUP
    source = lax.broadcasted_iota(jnp.int32, (rows, width), 0)
    place = lax.broadcasted_iota(jnp.int32, (rows, width), 1)
    expert = place // GROUP
    mine = source // block == (place // SLOTS) % 2
    named = jnp.zeros((rows, width), jnp.float32)
    scale = jnp.zeros((rows, width), jnp.float32)
    for choice in range(choices):
        same = jnp.logical_and(ids[:, choice : choice + 1] == expert, mine)
        named = jnp.where(same, 1.0, named)
        if scales is not None:
            scale = jnp.where(same, scales[:, choice : choice + 1], scale)
    row = lax.broadcasted_iota(jnp.int32, (rows, rows), 0)
    column = lax.broadcasted_iota(jnp.int32, (rows, rows), 1)
    before = jnp.where(column < row, 1.0, 0.0).astype(jnp.bfloat16)
    earlier = jnp.dot(before, named.astype(jnp.bfloat16), preferred_element_type=jnp.float32)
    chosen = jnp.logical_and(named > 0.0, earlier == (place % SLOTS).astype(jnp.float32))
    return jnp.where(chosen, named if scales is None else scale, 0.0)


def dispatch_kernel(step, kinds, counts, experts, section_ref, *refs):
    section = section_ref[0]
    gains, ids, refs = refs[:kinds], refs[kinds : 2 * kinds], refs[2 * kinds :]
    hidden_ref, out_ref = refs[-2:]
    layer = looked_up(LAYERS[step], section)
    gain = picked([ref[...] for ref in gains], layer)
    for lane, count in enumerate(counts):
        candidates, refs = refs[:count], refs[count:]
        hidden = picked([ref[...] for ref in candidates], looked_up(TAKES[step][lane], section))
        hidden_ref[lane] = hidden
        values = hidden.astype(jnp.float32)
        inverse = lax.rsqrt(jnp.mean(values * values, axis=-1, keepdims=True) + EPSILON)
        normed = (values * inverse * gain).astype(jnp.bfloat16)
        pair = looked_up(PAIRS[step][lane], section)
        placing = chosen_places(of_pair(ids, layer, pair), experts).T.astype(jnp.bfloat16)
        sent = jnp.dot(placing, normed, preferred_element_type=jnp.float32)
        out_ref[:, lane] = sent.astype(jnp.bfloat16).reshape(experts, GROUP, sent.shape[-1])


def pieces(features, units, width):
    panels = units // width
    order = [number for panel in range(panels) for number in (panel, panels + panel)]
    spans = [(number * features, features) for number in order]
    first = 2 * panels * features
    return spans + [(first + panel * units, units) for panel in range(features // width)]


def spread(refs, start, size):
    for ref in refs:
        if start < ref.shape[0]:
            return ref.at[pl.ds(start, size), :]
        start -= ref.shape[0]


def pack_kernel(width, outputs, *refs):
    out_refs, done = refs[-1 - outputs : -1], refs[-1]
    copies, start = [], 0
    for ref in refs[:3]:
        for column in range(0, ref.shape[1], width):
            to = spread(out_refs, start, ref.shape[0])
            copies.append(pltpu.make_async_copy(ref.at[:, pl.ds(column, width)], to, done.at[len(copies)]))
            start += ref.shape[0]
    for copy in copies:
        copy.start()
    for copy in copies:
        copy.wait()


def tables_kernel(kinds, experts, section_ref, *refs):
    section = section_ref[0]
    gains, ids, raw = refs[:kinds], refs[kinds : 2 * kinds], refs[2 * kinds : 3 * kinds]
    outs = iter(refs[3 * kinds :])
    for step in range(1, len(PAIRS)):
        gain_ref, placing_ref, scale_ref = next(outs), next(outs), next(outs)
        layer = looked_up(LAYERS[step], section)
        gain_ref[...] = picked([ref[...] for ref in gains], layer)
        for lane, table in enumerate(PAIRS[step]):
            pair = looked_up(table, section)
            named = of_pair(ids, layer, pair)
            weights = of_pair(raw, layer, pair)
            weights = weights / jnp.sum(weights, axis=-1, keepdims=True)
            placing_ref[lane] = chosen_places(named, experts).T.astype(jnp.bfloat16)
            scale = chosen_places(named, experts, weights)
            high = scale.astype(jnp.bfloat16)
            scale_ref[lane, 0] = high
            scale_ref[lane, 1] = (scale - high.astype(jnp.float32)).astype(jnp.bfloat16)


def dispatch_by_table_kernel(step, counts, section_ref, gain_ref, placing_ref, *refs):
    section = section_ref[0]
    hidden_ref, out_ref = refs[-2:]
    for lane, count in enumerate(counts):
        candidates, refs = refs[:count], refs[count:]
        hidden = picked([ref[...] for ref in candidates], looked_up(TAKES[step][lane], section))
        hidden_ref[lane] = hidden
        values = hidden.astype(jnp.float32)
        inverse = lax.rsqrt(jnp.mean(values * values, axis=-1, keepdims=True) + EPSILON)
        normed = (values * inverse * gain_ref[...]).astype(jnp.bfloat16)
        sent = jnp.dot(placing_ref[lane], normed, preferred_element_type=jnp.float32)
        out_ref[:, lane] = sent.astype(jnp.bfloat16).reshape(out_ref.shape[0], GROUP, sent.shape[-1])


def combine_by_table_kernel(last, section_ref, back_ref, hidden_ref, scale_ref, *refs):
    experts, lanes, _, features = back_ref.shape
    outs = refs[-lanes:]
    for lane in range(lanes):
        back = back_ref[:, lane].reshape(experts * GROUP, features)
        mixed = jnp.dot(scale_ref[lane, 0], back, preferred_element_type=jnp.float32)
        mixed += jnp.dot(scale_ref[lane, 1], back, preferred_element_type=jnp.float32)
        made = (hidden_ref[lane].astype(jnp.float32) + mixed).astype(jnp.bfloat16)
        if last is None:
            outs[lane][...] = made
        else:
            made = jnp.where(section_ref[0] == last, refs[0][...], made)
            block = made.shape[0] // 2
            outs[lane][0] = made[block:]
            outs[lane][1] = made[:block]


def ffn_kernel(step, given, held, section_ref, rows_ref, *refs):
    layers, refs = [refs[2 * number : 2 * number + 2] for number in range(held)], refs[2 * held :]
    out_ref, weights, activated, flat, arrived = refs[-5:]
    experts, lanes, _, features = rows_ref.shape
    units = activated.shape[-1]
    width = weights.shape[1]
    panels = units // width
    section = section_ref[0]
    spans = pieces(features, units, width)

    def copies(parts):
        for number, (start, size) in enumerate(spans):
            to = weights.at[pl.ds(start, size), :]
            yield pltpu.make_async_copy(spread(parts, start, size), to, arrived.at[number])

    if held == 1:
        for copy in copies(layers[0]):
            copy.start()
    else:
        layer = looked_up(LAYERS[step], section)
        layer = jnp.where(jnp.logical_and(layer == LOWER, section == 0), LOWER + 1, layer)
        for number, held_parts in enumerate(layers):

            @pl.when(layer == number)
            def _(held_parts=held_parts):
                for copy in copies(held_parts):
                    copy.start()

    def arrival(number, start, size):
        to = weights.at[pl.ds(pl.multiple_of(start, width), size), :]
        pltpu.make_async_copy(to, to, arrived.at[number]).wait()

    for lane in range(lanes):
        flat[lane] = rows_ref[:, lane].reshape(flat.shape[1:])

    def widen(panel, _):
        start = panel * features
        arrival(2 * panel, start, features)
        arrival(2 * panel + 1, start + panels * features, features)
        gates = weights[pl.ds(pl.multiple_of(start, width), features)]
        ups = weights[pl.ds(pl.multiple_of(start + panels * features, width), features)]
        part = pl.ds(pl.multiple_of(panel * width, width), width)
        for lane in range(lanes):
            gate = jnp.dot(flat[lane], gates, preferred_element_type=jnp.float32)
            up = jnp.dot(flat[lane], ups, preferred_element_type=jnp.float32)
            activated[lane, :, part] = (gate / (1.0 + jnp.exp(-gate)) * up).astype(jnp.bfloat16)
        return 0

    lax.fori_loop(0, panels, widen, 0)
    def narrow(panel, _):
        first = 2 * panels * features + panel * units
        arrival(2 * panels + panel, first, units)
        down = weights[pl.ds(pl.multiple_of(first, width), units)]
        part = pl.ds(pl.multiple_of(panel * width, width), width)
        for lane in range(lanes):
            made = jnp.dot(activated[lane], down, preferred_element_type=jnp.float32)
            made = made.astype(jnp.bfloat16).reshape(experts, GROUP, width)
            if given is not None and lane == lanes - 1:
                made = jnp.where(section == given, refs[0][:, 0, :, part], made)
            out_ref[:, lane, :, part] = made
        return 0

    lax.fori_loop(0, features // width, narrow, 0)


def combine_kernel(step, kinds, experts, last, section_ref, back_ref, hidden_ref, *refs):
    section = section_ref[0]
    ids, raw = refs[:kinds], refs[kinds : 2 * kinds]
    layer = looked_up(LAYERS[step], section)
    features = back_ref.shape[-1]
    lanes = back_ref.shape[1]
    outs = refs[-lanes:]
    for lane in range(lanes):
        pair = looked_up(PAIRS[step][lane], section)
        weights = of_pair(raw, layer, pair)
        weights = weights / jnp.sum(weights, axis=-1, keepdims=True)
        scale = chosen_places(of_pair(ids, layer, pair), experts, weights)
        high = scale.astype(jnp.bfloat16)
        low = (scale - high.astype(jnp.float32)).astype(jnp.bfloat16)
        back = back_ref[:, lane].reshape(experts * GROUP, features)
        mixed = jnp.dot(high, back, preferred_element_type=jnp.float32)
        mixed += jnp.dot(low, back, preferred_element_type=jnp.float32)
        made = (hidden_ref[lane].astype(jnp.float32) + mixed).astype(jnp.bfloat16)
        if last is None:
            outs[lane][...] = made
        else:
            made = jnp.where(section == last, refs[2 * kinds][...], made)
            block = made.shape[0] // 2
            outs[lane][0] = made[block:]
            outs[lane][1] = made[:block]


VMEM = pl.BlockSpec(memory_space=pltpu.VMEM)
SMEM = pl.BlockSpec(memory_space=pltpu.SMEM)
WHEREVER = pl.BlockSpec(memory_space=pl.ANY)


def limit(mebibytes):
    return pltpu.CompilerParams(vmem_limit_bytes=mebibytes * 1024 * 1024)


def dispatch(step, experts, section, gains, ids, lanes, ties=()):
    rows, features = lanes[0][0].shape
    counts = tuple(len(lane) for lane in lanes)
    operands = (*gains, *ids, *(value for lane in lanes for value in lane))
    return pl.pallas_call(
        functools.partial(dispatch_kernel, step, len(gains), counts, experts),
        out_shape=(
            jax.ShapeDtypeStruct((len(lanes), rows, features), jnp.bfloat16),
            jax.ShapeDtypeStruct((experts, len(lanes), GROUP, features), jnp.bfloat16),
        ),
        in_specs=[SMEM] + [VMEM] * len(operands) + [WHEREVER] * len(ties),
        out_specs=(VMEM, VMEM),
        compiler_params=limit(12),
    )(section, *operands, *ties)


def tables(experts, section, gains, ids, raw):
    rows = 2 * ids[0].shape[1]
    width = experts * GROUP
    shapes = []
    for lanes in map(len, PAIRS[1:]):
        shapes.append(jax.ShapeDtypeStruct(gains[0].shape, jnp.float32))
        shapes.append(jax.ShapeDtypeStruct((lanes, width, rows), jnp.bfloat16))
        shapes.append(jax.ShapeDtypeStruct((lanes, 2, rows, width), jnp.bfloat16))
    made = pl.pallas_call(
        functools.partial(tables_kernel, len(gains), experts),
        out_shape=tuple(shapes),
        in_specs=[SMEM] + [VMEM] * (3 * len(gains)),
        out_specs=tuple(VMEM for _ in shapes),
        cost_estimate=pl.CostEstimate(flops=LONG // 4, bytes_accessed=4096, transcendentals=0),
        compiler_params=limit(12),
    )(section, *gains, *ids, *raw)
    return [None] + [made[start : start + 3] for start in range(0, len(made), 3)]


def dispatch_by_table(step, experts, section, table, lanes, ties=()):
    rows, features = lanes[0][0].shape
    counts = tuple(len(lane) for lane in lanes)
    operands = (*table[:2], *(value for lane in lanes for value in lane))
    return pl.pallas_call(
        functools.partial(dispatch_by_table_kernel, step, counts),
        out_shape=(
            jax.ShapeDtypeStruct((len(lanes), rows, features), jnp.bfloat16),
            jax.ShapeDtypeStruct((experts, len(lanes), GROUP, features), jnp.bfloat16),
        ),
        in_specs=[SMEM] + [VMEM] * len(operands) + [WHEREVER] * len(ties),
        out_specs=(VMEM, VMEM),
        compiler_params=limit(12),
    )(section, *operands, *ties)


def combine_by_table(section, back, hidden, table, ties=(), last=None, finished=()):
    lanes, rows, features = hidden.shape
    shape = (rows, features) if last is None else (2, rows // 2, features)
    operands = (back, hidden, table[2], *finished)
    return pl.pallas_call(
        functools.partial(combine_by_table_kernel, last),
        out_shape=tuple(jax.ShapeDtypeStruct(shape, jnp.bfloat16) for _ in range(lanes)),
        in_specs=[SMEM] + [VMEM] * len(operands) + [WHEREVER] * len(ties),
        out_specs=tuple(VMEM for _ in range(lanes)),
        compiler_params=limit(12),
    )(section, *operands, *ties)


def token_kernel(*refs):
    refs[-1][...] = jnp.zeros_like(refs[-1])


def arrived_token(flops, *values):
    return pl.pallas_call(
        token_kernel,
        out_shape=jax.ShapeDtypeStruct((8, 128), jnp.float32),
        in_specs=[WHEREVER] * len(values),
        out_specs=VMEM,
        cost_estimate=pl.CostEstimate(flops=flops, bytes_accessed=4096, transcendentals=0),
        compiler_params=limit(4),
    )(*values)


def packed(gate, up, down, ties):
    features, units = gate.shape
    width = 256 if units % 256 == 0 and features % 256 == 0 else units
    panels = features // width
    ahead = panels - panels * 3 // 8
    rows = (2 * features * units // width + ahead * units, (panels - ahead) * units)
    return pl.pallas_call(
        functools.partial(pack_kernel, width, 2),
        out_shape=tuple(jax.ShapeDtypeStruct((count, width), gate.dtype) for count in rows),
        in_specs=[WHEREVER] * (3 + len(ties)),
        out_specs=(WHEREVER, WHEREVER),
        scratch_shapes=[pltpu.SemaphoreType.DMA((2 * units // width + panels,))],
        compiler_params=limit(4),
    )(gate, up, down, *ties)


def ffn(step, section, rows, layers, given=None, made=(), ties=()):
    experts, lanes, group, features = rows.shape
    width = layers[0][0].shape[1]
    length = sum(part.shape[0] for part in layers[0])
    held = len(layers)
    layers = [part for parts in layers for part in parts]
    units = length * width // (3 * features)
    height = experts * group
    return pl.pallas_call(
        functools.partial(ffn_kernel, step, given, held),
        out_shape=jax.ShapeDtypeStruct(rows.shape, jnp.bfloat16),
        in_specs=[SMEM, VMEM] + [WHEREVER] * len(layers) + [VMEM] * len(made) + [WHEREVER] * len(ties),
        out_specs=VMEM,
        scratch_shapes=[
            pltpu.VMEM((length, width), jnp.bfloat16),
            pltpu.VMEM((lanes, height, units), jnp.bfloat16),
            pltpu.VMEM((lanes, height, features), jnp.bfloat16),
            pltpu.SemaphoreType.DMA((len(pieces(features, units, width)),)),
        ],
        cost_estimate=pl.CostEstimate(
            flops=6 * lanes * height * features * units,
            bytes_accessed=6 * features * units + 4 * lanes * height * features,
            transcendentals=lanes * height * units,
        ),
        compiler_params=limit(28),
    )(section, rows, *layers, *made, *ties)


def combine(step, experts, section, back, hidden, ids, raw, ties=(), last=None, finished=()):
    lanes, rows, features = hidden.shape
    shape = (rows, features) if last is None else (2, rows // 2, features)
    operands = (back, hidden, *ids, *raw, *finished)
    return pl.pallas_call(
        functools.partial(combine_kernel, step, len(ids), experts, last),
        out_shape=tuple(jax.ShapeDtypeStruct(shape, jnp.bfloat16) for _ in range(lanes)),
        in_specs=[SMEM] + [VMEM] * len(operands) + [WHEREVER] * len(ties),
        out_specs=tuple(VMEM for _ in range(lanes)),
        compiler_params=limit(12),
    )(section, *operands, *ties)


def on_device(tokens, norm_gain, gate_proj, up_proj, down_proj, expert_ids, gate_weights):
    section = lax.axis_index("section")
    at = section.reshape(1)
    experts = lax.axis_size("expert")
    block, features = tokens.shape[1:]
    own = tokens.reshape(2 * block, features)

    def move(value, *route):
        return lax.ppermute(value, "section", route)

    def exchange(value):
        return lax.all_to_all(value, "expert", split_axis=0, concat_axis=0, tiled=True)

    downward = ((1, 0), (2, 1), (3, 2), (0, 3))
    upward = ((1, 2), (2, 3), (3, 0), (0, 1))
    small = (norm_gain, expert_ids[0], gate_weights[0])
    small_upper = tuple(move(value, *downward) for value in small)
    small_lower = tuple(move(value, *upward) for value in small)
    gains, ids, raw = zip(small, small_upper, small_lower)

    weights = (gate_proj[0, 0], up_proj[0, 0], down_proj[0, 0])

    first_in = move(own, (2, 0))
    second_in = move(own, (1, 0))
    hidden, sent = dispatch(0, experts, at, gains[:2], ids[:2], [(own, first_in)])
    layer = packed(*weights, (hidden, second_in, *small_upper, *small_lower))
    upper = [move(part, *downward[:3]) for part in layer]
    lower_early = [move(part, *upward[:2]) for part in layer]
    lower_late = [move(part, upward[2]) for part in layer]
    rows = exchange(sent)
    away = move(rows, (3, 0))
    made = exchange(ffn(0, at, rows, [layer]))
    table = tables(experts, at, gains, ids, raw)
    (state,) = combine(0, experts, at, made, hidden, ids[:1], raw[:1], (away, table[1][0]))
    state = move(state, (0, 1))

    away = move(ffn(0, at, away, [layer]), (0, 3))
    hidden, sent = dispatch_by_table(1, experts, at, table[1], [(own,), (own, second_in, state)])
    made = ffn(1, at, exchange(sent), [layer], 3, (away,))
    here = arrived_token(LONGER, upper[0], lower_early[0])
    kept, state = combine_by_table(at, exchange(made), hidden, table[1], (here,))
    state = move(state, (0, 1), (1, 3), (3, 2))

    layers = [layer, upper, lower_early]
    hidden, sent = dispatch_by_table(2, experts, at, table[2], [(state, kept)])
    made = exchange(ffn(2, at, exchange(sent), layers))
    here = arrived_token(LONG, *lower_late)
    (kept,) = combine_by_table(at, made, hidden, table[2], (here,))
    state = move(kept, (0, 3), (3, 0))

    layers.append(lower_late)
    hidden, sent = dispatch_by_table(3, experts, at, table[3], [(state, kept)])
    made = exchange(ffn(3, at, exchange(sent), layers))
    (kept,) = combine_by_table(at, made, hidden, table[3])
    state = move(kept, (1, 0), (0, 1))

    hidden, sent = dispatch_by_table(4, experts, at, table[4], [(state, kept)])
    made = exchange(ffn(4, at, exchange(sent), layers))
    (finished,) = combine_by_table(at, made, hidden, table[4], (), 1, (state,))
    return finished


def solution(mesh):
    return jax.shard_map(
        on_device,
        mesh=mesh,
        in_specs=(
            P("section", "expert", None),
            P("section", None),
            P("section", "expert", None, None),
            P("section", "expert", None, None),
            P("section", "expert", None, None),
            P("section", None, "expert", None),
            P("section", None, "expert", None),
        ),
        out_specs=P("section", "expert", None),
        check_vma=False,
    )
```
